256 devices in a mesh: dp: 16 (over z, core), row: 4 (over y), col: 4 (over x).
Axes of the slice: x: 4, y: 4, z: 8, core: 2. Of those that a mesh axis runs over, the one named last changes fastest.
Arguments:
- grad_parts: bfloat16 [16, 16, 256, 10240], P('dp', None, 'row', 'col'), may hold values from -64 to 64
- row_old: float32 [16, 256], P('dp', 'row'), may hold values from 0.1 to 2
- col_old: float32 [10240], P('col'), may hold values from 0.1 to 2
Outputs:
- update: float32 [16, 256, 10240], P('dp', 'row', 'col')
- row_new: float32 [16, 256], P('dp', 'row')
- col_new: float32 [10240], P('col')
- update_rms: float32 [], replicated
The draws below stay inside these ranges and needn't reach their ends.
All inputs are finite; a program needn't handle non-finite values.
Results may differ from the reference program's by a relative error of at most 0.0003.
Values sent between devices are 32-bit elements; how exact they have to be, the bound alone decides.
No kernel may reach another device: no remote copies, remote signals or barrier semaphores. Data moves between devices by JAX's collectives and lax.ppermute only.
A program may use at most 64 MiB of HBM per device.

```python
import math
import jax
import jax.numpy as jnp
from jax import lax

D = 4096
FF = 10240
BLOCK = 256
N_DP = 16


def draw_grad_parts(key, part):
    key = jax.random.fold_in(key, 7)
    k_noise, k_rows, k_cols = jax.random.split(key, 3)
    shape = (N_DP, N_DP, D // N_DP, FF)
    position = (jnp.arange(N_DP)[:, None] * (D // N_DP) + jnp.arange(D // N_DP)[None, :]).astype(jnp.float32) / (D - 1)
    row_scale = 10.0 ** (jax.random.uniform(k_rows, (N_DP, D // N_DP), jnp.float32) - 0.5) * 3.0 ** (position - 0.5)
    col_place = jnp.arange(FF).astype(jnp.float32) / (FF - 1)
    col_scale = 10.0 ** (jax.random.uniform(k_cols, (FF,), jnp.float32) - 0.5) * 3.0 ** (col_place - 0.5)
    replica = 3.0 ** (jnp.arange(N_DP).astype(jnp.float32) / max(N_DP - 1, 1)) / 1.8
    noise = jax.random.truncated_normal(k_noise, -4.0, 4.0, shape, jnp.float32)
    factor = 0.25
    value = factor * noise * replica[:, None, None, None] * row_scale[None, :, :, None] * col_scale[None, None, None, :]
    return value.astype(jnp.bfloat16)


def steps_of(key, extent, cuts, low, top_value):
    factor_of, own = 1.0, jax.random.fold_in(key, 6)
    for dim, blocks in cuts:
        heights = jnp.exp(jax.random.uniform(jax.random.fold_in(own, dim), (blocks,), jnp.float32, low / len(cuts), top_value / len(cuts)))
        factor_of = factor_of * jnp.repeat(heights, extent[dim] // blocks).reshape([-1 if axis == dim else 1 for axis in range(len(extent))])
    return factor_of


def setup_inputs(seed: int = 0) -> dict:
    arg_keys = jax.random.split(jax.random.key(seed), 4)
    return {
        "grad_parts": draw_grad_parts(jax.random.fold_in(arg_keys[3], 71), 0),
        "row_old": jnp.clip(jnp.exp(math.log(2.0) - 2.9957323 * jax.random.uniform(arg_keys[1], (N_DP, BLOCK), jnp.float32) ** steps_of(arg_keys[1], (N_DP, BLOCK), ((0, 16), (1, 4)), -0.2, 0.2)), 0.1, 2.0),
        "col_old": jnp.clip(jnp.exp(math.log(2.0) - 2.9957323 * jax.random.uniform(arg_keys[2], (FF,), jnp.float32) ** steps_of(arg_keys[2], (FF,), ((0, 4),), -0.2, 0.2)), 0.1, 2.0),
    }


def reference(grad_parts, row_old, col_old):

    def add_part(index, total):
        return total + grad_parts[index].astype(jnp.float32)
    grad = lax.fori_loop(0, N_DP, add_part, jnp.zeros((N_DP, D // N_DP, FF), jnp.float32))
    square = grad * grad + 1e-30
    row_new = 0.8 * row_old + 0.2 * lax.optimization_barrier(jnp.sum(square, axis=2)) / FF
    col_new = 0.8 * col_old + 0.2 * lax.optimization_barrier(jnp.sum(square, axis=(0, 1))) / D
    row_mean = jnp.sum(row_new) / D
    scaled = grad * jnp.sqrt(row_mean / (row_new[:, :, None] * col_new[None, None, :]))
    update_rms = jnp.sqrt(jnp.sum(scaled * scaled) / (D * FF))
    update = scaled / jnp.maximum(1.0, update_rms)
    return (update, row_new, col_new, update_rms)
```

```python
import functools

import jax
import jax.numpy as jnp
from jax import lax
from jax.experimental import pallas as pl
from jax.experimental.pallas import tpu as pltpu
from jax.sharding import PartitionSpec as P

D = 4096
FF = 10240
HALF = 32
ROWS = 64
COLS = 2560
ORDER = (2, 3, 1)

SWAP = [(i, i ^ 1) for i in range(16)]
UP = [(i, (i + 2) % 16) for i in range(16)]
DOWN = [(i, (i - 2) % 16) for i in range(16)]

VMEM = pl.BlockSpec(memory_space=pltpu.VMEM)
HBM = pl.BlockSpec(memory_space=pltpu.HBM)
ANY = pl.BlockSpec(memory_space=pl.ANY)
PARAMS = pltpu.CompilerParams(vmem_limit_bytes=8 * 1024 * 1024)


def told(micros):
    return pl.CostEstimate(flops=int(micros * 1.15e9), bytes_accessed=0, transcendentals=0)


def fetch_kernel(ks, n_in, parts, *refs):
    own, sent, buf, own_sems, sems = refs[n_in:]
    me = lax.axis_index("dp")
    core = jnp.bitwise_and(me, 1)
    own_copies, copies = [], []
    for i, k in enumerate(ks):
        dest = 2 * jnp.bitwise_and(lax.shift_right_logical(me, 1) + (k + 8), 7)
        copies.append(pltpu.make_async_copy(parts.at[dest + 1 - core], buf.at[i], sems.at[i]))
        own_copies.append(pltpu.make_async_copy(parts.at[dest + core], own.at[i], own_sems.at[i]))
    for copy in copies + own_copies:
        copy.start()
    for i, copy in enumerate(copies):
        copy.wait()
        sent[i] = buf[i].astype(jnp.float32)
    for copy in own_copies:
        copy.wait()


def fetch(ks, parts, *after, micros=0):
    n = len(ks)
    own, sent = pl.pallas_call(
        functools.partial(fetch_kernel, ks, len(after)),
        out_shape=[
            jax.ShapeDtypeStruct((n, ROWS, COLS), jnp.bfloat16),
            jax.ShapeDtypeStruct((n, ROWS, COLS), jnp.float32),
        ],
        in_specs=[HBM] + [ANY] * len(after),
        out_specs=[VMEM, VMEM],
        scratch_shapes=[
            pltpu.VMEM((n, ROWS, COLS), jnp.bfloat16),
            pltpu.SemaphoreType.DMA((n,)),
            pltpu.SemaphoreType.DMA((n,)),
        ],
        compiler_params=PARAMS,
        cost_estimate=told(micros),
    )(parts, *after)
    return own, lax.ppermute(sent, "dp", SWAP)


def add_kernel(terms, n_in, own, sib, *refs):
    outs = refs[n_in:]
    for i, (block, half, has_state) in enumerate(terms):
        rows = slice(half * HALF, (half + 1) * HALF)
        total = own[block, rows].astype(jnp.float32) + sib[block, rows]
        if has_state:
            total = total + refs[i][...]
        outs[i][...] = total


def add(blocks, terms, states=(), after=(), micros=40):
    return pl.pallas_call(
        functools.partial(add_kernel, [(*t, bool(states)) for t in terms], len(states) + len(after)),
        out_shape=[jax.ShapeDtypeStruct((HALF, COLS), jnp.float32)] * len(terms),
        in_specs=[VMEM] * (2 + len(states)) + [ANY] * len(after),
        out_specs=[VMEM] * len(terms),
        compiler_params=PARAMS,
        cost_estimate=told(micros),
    )(*blocks, *states, *after)


def final_kernel(scaled, row_sum, total, out, rms, buf, sems):
    row_mean = jnp.sum(row_sum[...], keepdims=True) / D
    update_rms = jnp.sqrt(row_mean * jnp.sum(total[...], keepdims=True) / (D * FF))
    rms[...] = update_rms
    factor = jnp.sqrt(row_mean) / jnp.maximum(1.0, update_rms)
    copies = []
    for i in range(4):
        rows = pl.ds(16 * i, 16)
        buf[rows] = scaled[rows] * factor
        copies.append(pltpu.make_async_copy(buf.at[rows], out.at[rows], sems.at[i]))
        copies[i].start()
    for copy in copies:
        copy.wait()


def final(scaled, row_sum, total):
    return pl.pallas_call(
        final_kernel,
        out_shape=[
            jax.ShapeDtypeStruct((ROWS, COLS), jnp.float32),
            jax.ShapeDtypeStruct((1, 1), jnp.float32),
        ],
        in_specs=[VMEM, VMEM, VMEM],
        out_specs=[HBM, VMEM],
        scratch_shapes=[pltpu.VMEM((ROWS, COLS), jnp.float32), pltpu.SemaphoreType.DMA((4,))],
        compiler_params=PARAMS,
        cost_estimate=told(1),
    )(scaled, row_sum, total)


def places():
    return [(z, c, y, x) for z in range(8) for c in range(2) for y in range(4) for x in range(4)]


def number(z, c, y, x):
    return ((2 * z + c) * 4 + y) * 4 + x


def exchange(v, mask, idle=None):
    pairs = []
    for z, c, y, x in places():
        dz, dy, dx = mask if c == 1 or idle is None else idle
        pairs.append((number(z, c, y, x), number(z ^ dz, c, y ^ dy, x ^ dx)))
    return lax.ppermute(v, ("dp", "row", "col"), pairs)


def sum_four(v, axis, idle=None):
    unit = [0, 0, 0]
    got = {}
    for mask in ORDER:
        unit[axis] = mask
        got[mask] = exchange(v, tuple(unit), idle)
    return (got[2] + got[3]) + (got[1] + v)


def on_device(grad_parts, row_old, col_old):
    parts = pltpu.with_memory_space_constraint(grad_parts[0], pltpu.HBM)
    core_one = jnp.bitwise_and(lax.axis_index("dp"), 1) == 1

    def up(x):
        return lax.ppermute(x, "dp", UP)

    def down(x):
        return lax.ppermute(x, "dp", DOWN)

    far = fetch((4,), parts)
    third = fetch((3, -3), parts, far[0], micros=40)
    a, b = add(far, ((0, 0), (0, 1)), after=(third[0],))
    after = a
    a, b = up(a), down(b)
    c, d = add(third, ((0, 1), (1, 0)), after=(after,))
    second = fetch((2, -2), parts, c)
    near = fetch((1, -1, 0), parts, second[0])
    c, d = up(c), down(d)
    a, b = add(third, ((0, 0), (1, 1)), (a, b), after=(near[0],))
    after = a
    a, b = up(a), down(b)
    c, d = add(second, ((0, 1), (1, 0)), (c, d), after=(after,))
    after = c
    c, d = up(c), down(d)
    a, b = add(second, ((0, 0), (1, 1)), (a, b), after=(after,))
    after = a
    a, b = up(a), down(b)
    c, d = add(near, ((0, 1), (1, 0)), (c, d), after=(after,))
    after = c
    c, d = up(c), down(d)
    a, b = add(near, ((0, 0), (1, 1)), (a, b), after=(after,))
    after = a
    a, b = up(a), down(b)
    upper, lower = add(near, ((2, 0), (2, 1)), (d, c), after=(after,))
    grad = jnp.concatenate([upper + a, lower + b], axis=0)

    square = grad * grad
    row_part = jnp.sum(square + 1e-30, axis=1)
    col_part = jnp.sum(square + 1e-30, axis=0)
    row_total = sum_four(row_part, 2)
    row_new = 0.8 * row_old[0] + 0.2 * row_total / FF
    weighted = jnp.sum(square * (1.0 / row_new)[:, None], axis=0)
    packed = jnp.concatenate([col_part, weighted, row_new, jnp.zeros((64,), jnp.float32)])

    packed = packed + lax.ppermute(packed, "dp", SWAP)
    packed = sum_four(packed, 0, (0, 0, 1))
    packed = packed + exchange(packed, (7, 0, 0), (0, 0, 1))
    packed = sum_four(packed, 1, (0, 0, 1))
    col_new = 0.8 * col_old + 0.2 * packed[:COLS] / D
    total = jnp.sum((packed[COLS:2 * COLS] / col_new).reshape(20, 128), axis=0)
    total = sum_four(total, 2, (0, 1, 0))
    core_one = jnp.bitwise_and(lax.axis_index("dp"), 1) == 1

    packed = jnp.concatenate([col_new, packed[2 * COLS:], total])
    packed = jnp.where(core_one, packed, lax.ppermute(packed, "dp", SWAP))
    col_new, row_sum, total = packed[:COLS], packed[COLS:COLS + 128], packed[COLS + 128:]
    scaled = grad * lax.rsqrt(row_new[:, None] * col_new[None, :])
    update, update_rms = final(scaled, row_sum.reshape(1, 128), total.reshape(1, 128))
    return (update[None], row_new[None], col_new, update_rms.reshape(()))


def solution(mesh):
    return jax.shard_map(
        on_device,
        mesh=mesh,
        in_specs=(P("dp", None, "row", "col"), P("dp", "row"), P("col")),
        out_specs=(P("dp", "row", "col"), P("dp", "row"), P("col"), P()),
        check_vma=False,
    )
```

```python
import functools

import jax
import jax.numpy as jnp
from jax import lax
from jax.experimental import pallas as pl
from jax.experimental.pallas import tpu as pltpu
from jax.sharding import PartitionSpec as P

D = 4096
FF = 10240
HALF = 32
ROWS = 64
COLS = 2560
ORDER = (2, 3, 1)

SWAP = [(i, i ^ 1) for i in range(16)]
UP = [(2 * z + c, 2 * ((z + 1 - 2 * c) % 8) + c) for z in range(8) for c in range(2)]
DOWN = [(j, i) for i, j in UP]

VMEM = pl.BlockSpec(memory_space=pltpu.VMEM)
HBM = pl.BlockSpec(memory_space=pltpu.HBM)
ANY = pl.BlockSpec(memory_space=pl.ANY)
PARAMS = pltpu.CompilerParams(vmem_limit_bytes=8 * 1024 * 1024)


def told(micros):
    return pl.CostEstimate(flops=int(micros * 1.15e9), bytes_accessed=0, transcendentals=0)


def fetch_kernel(ks, n_in, parts, *refs):
    own, sent, buf, own_sems, sems = refs[n_in:]
    me = lax.axis_index("dp")
    core = jnp.bitwise_and(me, 1)
    z = lax.shift_right_logical(me, 1) + 8
    own_copies, copies = [], []
    for i, k in enumerate(ks):
        step = k * (1 - 2 * core)
        here = 2 * jnp.bitwise_and(z + step, 7) + core
        there = 2 * jnp.bitwise_and(z - step, 7) + 1 - core
        copies.append(pltpu.make_async_copy(parts.at[there], buf.at[i], sems.at[i]))
        own_copies.append(pltpu.make_async_copy(parts.at[here], own.at[i], own_sems.at[i]))
    for copy in copies + own_copies:
        copy.start()
    for i, copy in enumerate(copies):
        copy.wait()
        sent[i] = buf[i].astype(jnp.float32)
    for copy in own_copies:
        copy.wait()


def fetch(ks, parts, *after, micros=0):
    n = len(ks)
    own, sent = pl.pallas_call(
        functools.partial(fetch_kernel, ks, len(after)),
        out_shape=[
            jax.ShapeDtypeStruct((n, ROWS, COLS), jnp.bfloat16),
            jax.ShapeDtypeStruct((n, ROWS, COLS), jnp.float32),
        ],
        in_specs=[HBM] + [ANY] * len(after),
        out_specs=[VMEM, VMEM],
        scratch_shapes=[
            pltpu.VMEM((n, ROWS, COLS), jnp.bfloat16),
            pltpu.SemaphoreType.DMA((n,)),
            pltpu.SemaphoreType.DMA((n,)),
        ],
        compiler_params=PARAMS,
        cost_estimate=told(micros),
    )(parts, *after)
    return own, lax.ppermute(sent, "dp", SWAP)


def add_kernel(terms, n_in, own, sib, *refs):
    outs = refs[n_in:]
    for i, (block, half, has_state) in enumerate(terms):
        rows = slice(half * HALF, (half + 1) * HALF)
        total = own[block, rows].astype(jnp.float32) + sib[block, rows]
        if has_state:
            total = total + refs[i][...]
        outs[i][...] = total


def add(blocks, terms, states=(), after=(), micros=40):
    return pl.pallas_call(
        functools.partial(add_kernel, [(*t, bool(states)) for t in terms], len(states) + len(after)),
        out_shape=[jax.ShapeDtypeStruct((HALF, COLS), jnp.float32)] * len(terms),
        in_specs=[VMEM] * (2 + len(states)) + [ANY] * len(after),
        out_specs=[VMEM] * len(terms),
        compiler_params=PARAMS,
        cost_estimate=told(micros),
    )(*blocks, *states, *after)


def final_kernel(scaled, row_sum, total, out, rms, buf, sems):
    row_mean = jnp.sum(row_sum[...], keepdims=True) / D
    update_rms = jnp.sqrt(row_mean * jnp.sum(total[...], keepdims=True) / (D * FF))
    rms[...] = update_rms
    factor = jnp.sqrt(row_mean) / jnp.maximum(1.0, update_rms)
    copies = []
    for i in range(4):
        rows = pl.ds(16 * i, 16)
        buf[rows] = scaled[rows] * factor
        copies.append(pltpu.make_async_copy(buf.at[rows], out.at[rows], sems.at[i]))
        copies[i].start()
    for copy in copies:
        copy.wait()


def final(scaled, row_sum, total):
    return pl.pallas_call(
        final_kernel,
        out_shape=[
            jax.ShapeDtypeStruct((ROWS, COLS), jnp.float32),
            jax.ShapeDtypeStruct((1, 1), jnp.float32),
        ],
        in_specs=[VMEM, VMEM, VMEM],
        out_specs=[HBM, VMEM],
        scratch_shapes=[pltpu.VMEM((ROWS, COLS), jnp.float32), pltpu.SemaphoreType.DMA((4,))],
        compiler_params=PARAMS,
        cost_estimate=told(1),
    )(scaled, row_sum, total)


def places():
    return [(z, c, y, x) for z in range(8) for c in range(2) for y in range(4) for x in range(4)]


def number(z, c, y, x):
    return ((2 * z + c) * 4 + y) * 4 + x


def exchange(v, mask, idle=None):
    pairs = []
    for z, c, y, x in places():
        dz, dy, dx = mask if c == 1 or idle is None else idle
        pairs.append((number(z, c, y, x), number(z ^ dz, c, y ^ dy, x ^ dx)))
    return lax.ppermute(v, ("dp", "row", "col"), pairs)


def sum_four(v, axis, idle=None):
    unit = [0, 0, 0]
    got = {}
    for mask in ORDER:
        unit[axis] = mask
        got[mask] = exchange(v, tuple(unit), idle)
    return (got[2] + got[3]) + (got[1] + v)


def on_device(grad_parts, row_old, col_old):
    parts = pltpu.with_memory_space_constraint(grad_parts[0], pltpu.HBM)
    core_one = jnp.bitwise_and(lax.axis_index("dp"), 1) == 1

    def up(x):
        return lax.ppermute(x, "dp", UP)

    def down(x):
        return lax.ppermute(x, "dp", DOWN)

    far = fetch((4,), parts)
    third = fetch((3, -3), parts, far[0], micros=40)
    a, b = add(far, ((0, 0), (0, 1)), after=(third[0],))
    after = a
    a, b = up(a), down(b)
    c, d = add(third, ((0, 1), (1, 0)), after=(after,))
    second = fetch((2, -2), parts, c)
    near = fetch((1, -1, 0), parts, second[0])
    c, d = up(c), down(d)
    a, b = add(third, ((0, 0), (1, 1)), (a, b), after=(near[0],))
    after = a
    a, b = up(a), down(b)
    c, d = add(second, ((0, 1), (1, 0)), (c, d), after=(after,))
    after = c
    c, d = up(c), down(d)
    a, b = add(second, ((0, 0), (1, 1)), (a, b), after=(after,))
    after = a
    a, b = up(a), down(b)
    c, d = add(near, ((0, 1), (1, 0)), (c, d), after=(after,))
    after = c
    c, d = up(c), down(d)
    a, b = add(near, ((0, 0), (1, 1)), (a, b), after=(after,))
    after = a
    a, b = up(a), down(b)
    upper, lower = add(near, ((2, 0), (2, 1)), (d, c), after=(after,))
    grad = jnp.concatenate([upper + a, lower + b], axis=0)

    square = grad * grad
    row_part = jnp.sum(square + 1e-30, axis=1)
    col_part = jnp.sum(square + 1e-30, axis=0)
    row_total = sum_four(row_part, 2)
    row_new = 0.8 * row_old[0] + 0.2 * row_total / FF
    weighted = jnp.sum(square * (1.0 / row_new)[:, None], axis=0)
    packed = jnp.concatenate([col_part, weighted, row_new, jnp.zeros((64,), jnp.float32)])

    packed = packed + lax.ppermute(packed, "dp", SWAP)
    packed = sum_four(packed, 0, (0, 0, 1))
    packed = packed + exchange(packed, (7, 0, 0), (0, 0, 1))
    packed = sum_four(packed, 1, (0, 0, 1))
    col_new = 0.8 * col_old + 0.2 * packed[:COLS] / D
    total = jnp.sum((packed[COLS:2 * COLS] / col_new).reshape(20, 128), axis=0)
    total = sum_four(total, 2, (0, 1, 0))
    core_one = jnp.bitwise_and(lax.axis_index("dp"), 1) == 1

    packed = jnp.concatenate([col_new, packed[2 * COLS:], total])
    packed = jnp.where(core_one, packed, lax.ppermute(packed, "dp", SWAP))
    col_new, row_sum, total = packed[:COLS], packed[COLS:COLS + 128], packed[COLS + 128:]
    scaled = grad * lax.rsqrt(row_new[:, None] * col_new[None, :])
    update, update_rms = final(scaled, row_sum.reshape(1, 128), total.reshape(1, 128))
    return (update[None], row_new[None], col_new, update_rms.reshape(()))


def solution(mesh):
    return jax.shard_map(
        on_device,
        mesh=mesh,
        in_specs=(P("dp", None, "row", "col"), P("dp", "row"), P("col")),
        out_specs=(P("dp", "row", "col"), P("dp", "row"), P("col"), P()),
        check_vma=False,
    )
```

```python
import functools

import jax
import jax.numpy as jnp
from jax import lax
from jax.experimental import pallas as pl
from jax.experimental.pallas import tpu as pltpu
from jax.sharding import PartitionSpec as P

D = 4096
FF = 10240
HALF = 32
ROWS = 64
COLS = 2560
ORDER = (2, 3, 1)

SWAP = [(i, i ^ 1) for i in range(16)]
UP = [(2 * z + c, 2 * ((z + 1 - 2 * c) % 8) + c) for z in range(8) for c in range(2)]
DOWN = [(j, i) for i, j in UP]

VMEM = pl.BlockSpec(memory_space=pltpu.VMEM)
HBM = pl.BlockSpec(memory_space=pltpu.HBM)
ANY = pl.BlockSpec(memory_space=pl.ANY)
PARAMS = pltpu.CompilerParams(vmem_limit_bytes=8 * 1024 * 1024)


def told(micros):
    return pl.CostEstimate(flops=int(micros * 1.15e9), bytes_accessed=0, transcendentals=0)


def fetch_kernel(ks, n_in, parts, *refs):
    own, sent, buf, own_sems, sems = refs[n_in:]
    me = lax.axis_index("dp")
    core = jnp.bitwise_and(me, 1)
    z = lax.shift_right_logical(me, 1) + 8
    own_copies, copies = [], []
    for i, k in enumerate(ks):
        step = k * (1 - 2 * core)
        here = 2 * jnp.bitwise_and(z + step, 7) + core
        there = 2 * jnp.bitwise_and(z - step, 7) + 1 - core
        copies.append(pltpu.make_async_copy(parts.at[there], buf.at[i], sems.at[i]))
        own_copies.append(pltpu.make_async_copy(parts.at[here], own.at[i], own_sems.at[i]))
    for copy in copies + own_copies:
        copy.start()
    for i, copy in enumerate(copies):
        copy.wait()
        sent[i] = buf[i].astype(jnp.float32)
    for copy in own_copies:
        copy.wait()


def fetch(ks, parts, *after, micros=0):
    n = len(ks)
    own, sent = pl.pallas_call(
        functools.partial(fetch_kernel, ks, len(after)),
        out_shape=[
            jax.ShapeDtypeStruct((n, ROWS, COLS), jnp.bfloat16),
            jax.ShapeDtypeStruct((n, ROWS, COLS), jnp.float32),
        ],
        in_specs=[HBM] + [ANY] * len(after),
        out_specs=[VMEM, VMEM],
        scratch_shapes=[
            pltpu.VMEM((n, ROWS, COLS), jnp.bfloat16),
            pltpu.SemaphoreType.DMA((n,)),
            pltpu.SemaphoreType.DMA((n,)),
        ],
        compiler_params=PARAMS,
        cost_estimate=told(micros),
    )(parts, *after)
    return own, lax.ppermute(sent, "dp", SWAP)


def add_kernel(terms, n_in, own, sib, *refs):
    outs = refs[n_in:]
    for i, (block, half, has_state) in enumerate(terms):
        rows = slice(half * HALF, (half + 1) * HALF)
        total = own[block, rows].astype(jnp.float32) + sib[block, rows]
        if has_state:
            total = total + refs[i][...]
        outs[i][...] = total


def add(blocks, terms, states=(), after=(), micros=40):
    return pl.pallas_call(
        functools.partial(add_kernel, [(*t, bool(states)) for t in terms], len(states) + len(after)),
        out_shape=[jax.ShapeDtypeStruct((HALF, COLS), jnp.float32)] * len(terms),
        in_specs=[VMEM] * (2 + len(states)) + [ANY] * len(after),
        out_specs=[VMEM] * len(terms),
        compiler_params=PARAMS,
        cost_estimate=told(micros),
    )(*blocks, *states, *after)


def final_kernel(scaled, row_sum, total, out, rms, buf, sems):
    row_mean = jnp.sum(row_sum[...], keepdims=True) / D
    update_rms = jnp.sqrt(row_mean * jnp.sum(total[...], keepdims=True) / (D * FF))
    rms[...] = update_rms
    factor = jnp.sqrt(row_mean) / jnp.maximum(1.0, update_rms)
    copies = []
    for i in range(4):
        rows = pl.ds(16 * i, 16)
        buf[rows] = scaled[rows] * factor
        copies.append(pltpu.make_async_copy(buf.at[rows], out.at[rows], sems.at[i]))
        copies[i].start()
    for copy in copies:
        copy.wait()


def final(scaled, row_sum, total):
    return pl.pallas_call(
        final_kernel,
        out_shape=[
            jax.ShapeDtypeStruct((ROWS, COLS), jnp.float32),
            jax.ShapeDtypeStruct((1, 1), jnp.float32),
        ],
        in_specs=[VMEM, VMEM, VMEM],
        out_specs=[HBM, VMEM],
        scratch_shapes=[pltpu.VMEM((ROWS, COLS), jnp.float32), pltpu.SemaphoreType.DMA((4,))],
        compiler_params=PARAMS,
        cost_estimate=told(1),
    )(scaled, row_sum, total)


def places():
    return [(z, c, y, x) for z in range(8) for c in range(2) for y in range(4) for x in range(4)]


def number(z, c, y, x):
    return ((2 * z + c) * 4 + y) * 4 + x


def exchange(v, mask, idle=None):
    pairs = []
    for z, c, y, x in places():
        dz, dy, dx = mask if c == 1 or idle is None else idle
        pairs.append((number(z, c, y, x), number(z ^ dz, c, y ^ dy, x ^ dx)))
    return lax.ppermute(v, ("dp", "row", "col"), pairs)


def sum_four(v, axis, idle=None):
    unit = [0, 0, 0]
    got = {}
    for mask in ORDER:
        unit[axis] = mask
        got[mask] = exchange(v, tuple(unit), idle)
    return (got[2] + got[3]) + (got[1] + v)


def on_device(grad_parts, row_old, col_old):
    parts = pltpu.with_memory_space_constraint(grad_parts[0], pltpu.HBM)
    core_one = jnp.bitwise_and(lax.axis_index("dp"), 1) == 1

    def up(x):
        return lax.ppermute(x, "dp", UP)

    def down(x):
        return lax.ppermute(x, "dp", DOWN)

    far = fetch((4,), parts)
    third = fetch((3, -3), parts, far[0], micros=40)
    a, b = add(far, ((0, 0), (0, 1)), after=(third[0],))
    after = a
    a, b = up(a), down(b)
    c, d = add(third, ((0, 1), (1, 0)), after=(after,))
    second = fetch((2, -2), parts, c)
    near = fetch((1, -1, 0), parts, second[0])
    c, d = up(c), down(d)
    a, b = add(third, ((0, 0), (1, 1)), (a, b), after=(near[0],))
    after = a
    a, b = up(a), down(b)
    c, d = add(second, ((0, 1), (1, 0)), (c, d), after=(after,))
    after = c
    c, d = up(c), down(d)
    a, b = add(second, ((0, 0), (1, 1)), (a, b), after=(after,))
    after = a
    a, b = up(a), down(b)
    c, d = add(near, ((0, 1), (1, 0)), (c, d), after=(after,))
    after = c
    c, d = up(c), down(d)
    a, b = add(near, ((0, 0), (1, 1)), (a, b), after=(after,))
    after = a
    a, b = up(a), down(b)
    upper, lower = add(near, ((2, 0), (2, 1)), (d, c), after=(after,))
    grad = jnp.concatenate([upper + a, lower + b], axis=0)

    grad = lax.optimization_barrier(grad)
    row_own = jnp.concatenate([jnp.sum(grad * grad + 1e-30, axis=1), row_old[0]])
    row_other = lax.ppermute(row_own, "dp", SWAP)
    grad_other, row_other = lax.optimization_barrier((grad, row_other))
    grad_other = lax.ppermute(grad_other, "dp", SWAP)
    row_total = sum_four(jnp.concatenate([row_own[:ROWS], row_other[:ROWS]]), 2, (0, 1, 0))
    row_new = 0.8 * jnp.concatenate([row_own[ROWS:], row_other[ROWS:]]) + 0.2 * row_total / FF
    packed = []
    for weight in (None, 1.0 / row_new):
        sums = 0.0
        for g, rows in ((grad, slice(0, ROWS)), (grad_other, slice(ROWS, 2 * ROWS))):
            term = g * g + 1e-30 if weight is None else g * g * weight[rows, None]
            sums = sums + jnp.sum(term, axis=0)
        packed.append(sums)
    packed = jnp.concatenate([*packed, row_new])

    packed = sum_four(packed, 0, (0, 0, 1))
    packed = packed + exchange(packed, (7, 0, 0), (0, 0, 1))
    packed = sum_four(packed, 1, (0, 0, 1))
    col_new = 0.8 * col_old + 0.2 * packed[:COLS] / D
    total = jnp.sum((packed[COLS:2 * COLS] / col_new).reshape(20, 128), axis=0)
    total = sum_four(total, 2, (0, 1, 0))
    core_one = jnp.bitwise_and(lax.axis_index("dp"), 1) == 1

    packed = jnp.concatenate([col_new, packed[2 * COLS:], total, row_new])
    other = lax.ppermute(packed, "dp", SWAP)
    row_new = jnp.where(core_one, packed[-2 * ROWS:-ROWS], other[-ROWS:])
    packed = jnp.where(core_one, packed, other)
    col_new, row_sum, total = packed[:COLS], packed[COLS:COLS + 128], packed[COLS + 128:COLS + 256]
    scaled = grad * lax.rsqrt(row_new[:, None] * col_new[None, :])
    update, update_rms = final(scaled, row_sum.reshape(1, 128), total.reshape(1, 128))
    return (update[None], row_new[None], col_new, update_rms.reshape(()))


def solution(mesh):
    return jax.shard_map(
        on_device,
        mesh=mesh,
        in_specs=(P("dp", None, "row", "col"), P("dp", "row"), P("col")),
        out_specs=(P("dp", "row", "col"), P("dp", "row"), P("col"), P()),
        check_vma=False,
    )
```

```python
import functools

import jax
import jax.numpy as jnp
from jax import lax
from jax.experimental import pallas as pl
from jax.experimental.pallas import tpu as pltpu
from jax.sharding import PartitionSpec as P

D = 4096
FF = 10240
HALF = 32
ROWS = 64
COLS = 2560

SWAP = [(i, i ^ 1) for i in range(16)]
UP = [(2 * z + c, 2 * ((z + 1 - 2 * c) % 8) + c) for z in range(8) for c in range(2)]
DOWN = [(j, i) for i, j in UP]

VMEM = pl.BlockSpec(memory_space=pltpu.VMEM)
HBM = pl.BlockSpec(memory_space=pltpu.HBM)
ANY = pl.BlockSpec(memory_space=pl.ANY)
PARAMS = pltpu.CompilerParams(vmem_limit_bytes=8 * 1024 * 1024)


def told(micros):
    return pl.CostEstimate(flops=int(micros * 1.15e9), bytes_accessed=0, transcendentals=0)


def fetch_kernel(ks, split, n_in, parts, *refs):
    own, *sent = refs[n_in:-3]
    buf, own_sems, sems = refs[-3:]
    height = ROWS // split
    me = lax.axis_index("dp")
    core = jnp.bitwise_and(me, 1)
    z = lax.shift_right_logical(me, 1) + 8
    own_copies, copies = [], []
    for i, k in enumerate(ks):
        step = k * (1 - 2 * core)
        here = 2 * jnp.bitwise_and(z + step, 7) + core
        there = 2 * jnp.bitwise_and(z - step, 7) + 1 - core
        copies.append(pltpu.make_async_copy(parts.at[there], buf.at[i], sems.at[i]))
        own_copies.append(pltpu.make_async_copy(parts.at[here], own.at[i], own_sems.at[i]))
    for copy in copies + own_copies:
        copy.start()
    for i, copy in enumerate(copies):
        copy.wait()
        for j in range(split):
            sent[j][i] = buf[i, j * height:(j + 1) * height].astype(jnp.float32)
    for copy in own_copies:
        copy.wait()


def fetch(ks, parts, *after, split=1, micros=0):
    n = len(ks)
    own, *sent = pl.pallas_call(
        functools.partial(fetch_kernel, ks, split, len(after)),
        out_shape=[jax.ShapeDtypeStruct((n, ROWS, COLS), jnp.bfloat16)]
        + [jax.ShapeDtypeStruct((n, ROWS // split, COLS), jnp.float32)] * split,
        in_specs=[HBM] + [ANY] * len(after),
        out_specs=[VMEM] * (1 + split),
        scratch_shapes=[
            pltpu.VMEM((n, ROWS, COLS), jnp.bfloat16),
            pltpu.SemaphoreType.DMA((n,)),
            pltpu.SemaphoreType.DMA((n,)),
        ],
        compiler_params=PARAMS,
        cost_estimate=told(micros),
    )(parts, *after)
    return own, *(lax.ppermute(x, "dp", SWAP) for x in sent)


def add_kernel(terms, n_in, own, sib, *refs):
    outs = refs[n_in:]
    for i, (block, half, has_state) in enumerate(terms):
        rows = slice(half * HALF, (half + 1) * HALF)
        other = sib[block, rows] if sib.shape[1] == ROWS else sib[block]
        total = own[block, rows].astype(jnp.float32) + other
        if has_state:
            total = total + refs[i][...]
        outs[i][...] = total


def add(blocks, terms, states=(), after=(), micros=40):
    return pl.pallas_call(
        functools.partial(add_kernel, [(*t, bool(states)) for t in terms], len(states) + len(after)),
        out_shape=[jax.ShapeDtypeStruct((HALF, COLS), jnp.float32)] * len(terms),
        in_specs=[VMEM] * (2 + len(states)) + [ANY] * len(after),
        out_specs=[VMEM] * len(terms),
        compiler_params=PARAMS,
        cost_estimate=told(micros),
    )(*blocks, *states, *after)


def hold_kernel(x, _, out):
    out[...] = x[...]


def hold(x, after):
    return pl.pallas_call(
        hold_kernel,
        out_shape=jax.ShapeDtypeStruct(x.shape, x.dtype),
        in_specs=[VMEM, ANY],
        out_specs=VMEM,
        compiler_params=PARAMS,
        cost_estimate=told(0),
    )(x, after)


def final_kernel(scaled, row_sum, total, out, rms, buf, sems):
    row_mean = jnp.sum(row_sum[...], keepdims=True) / D
    update_rms = jnp.sqrt(row_mean * jnp.sum(total[...], keepdims=True) / (D * FF))
    rms[...] = update_rms
    factor = jnp.sqrt(row_mean) / jnp.maximum(1.0, update_rms)
    copies = []
    for i in range(4):
        rows = pl.ds(16 * i, 16)
        buf[rows] = scaled[rows] * factor
        copies.append(pltpu.make_async_copy(buf.at[rows], out.at[rows], sems.at[i]))
        copies[i].start()
    for copy in copies:
        copy.wait()


def final(scaled, row_sum, total):
    return pl.pallas_call(
        final_kernel,
        out_shape=[
            jax.ShapeDtypeStruct((ROWS, COLS), jnp.float32),
            jax.ShapeDtypeStruct((1, 1), jnp.float32),
        ],
        in_specs=[VMEM, VMEM, VMEM],
        out_specs=[HBM, VMEM],
        scratch_shapes=[pltpu.VMEM((ROWS, COLS), jnp.float32), pltpu.SemaphoreType.DMA((4,))],
        compiler_params=PARAMS,
        cost_estimate=told(1),
    )(scaled, row_sum, total)


def places():
    return [(z, c, y, x) for z in range(8) for c in range(2) for y in range(4) for x in range(4)]


def number(z, c, y, x):
    return ((2 * z + c) * 4 + y) * 4 + x


def exchange(v, mask, idle=None):
    pairs = []
    for z, c, y, x in places():
        dz, dy, dx = mask if c == 1 or idle is None else idle
        pairs.append((number(z, c, y, x), number(z ^ dz, c, y ^ dy, x ^ dx)))
    return lax.ppermute(v, ("dp", "row", "col"), pairs)


def sum_four(v, axis, idle=None, masks=(2, 3, 1)):
    unit = [0, 0, 0]
    got = []
    for mask in masks:
        unit[axis] = mask
        got.append(exchange(v, tuple(unit), idle))
    return (got[0] + got[1]) + (got[2] + v)


def on_device(grad_parts, row_old, col_old):
    parts = pltpu.with_memory_space_constraint(grad_parts[0], pltpu.HBM)
    core_one = jnp.bitwise_and(lax.axis_index("dp"), 1) == 1

    def up(x):
        return lax.ppermute(x, "dp", UP)

    def down(x):
        return lax.ppermute(x, "dp", DOWN)

    far, far_up, far_down = fetch((4,), parts, split=2)
    third = fetch((3, -3), parts, far, micros=40)
    (a,) = add((far, far_up), ((0, 0),), after=(third[0],))
    after = a
    a = up(a)
    (b,) = add((far, far_down), ((0, 1),), after=(after,))
    after = b
    b = down(b)
    c, d = add(third, ((0, 1), (1, 0)), after=(after,))
    second = fetch((2, -2), parts, c)
    near = fetch((1, -1, 0), parts, second[0])
    c, d = up(c), down(d)
    a, b = add(third, ((0, 0), (1, 1)), (a, b), after=(near[0],))
    after = a
    a, b = up(a), down(b)
    c, d = add(second, ((0, 1), (1, 0)), (c, d), after=(after,))
    after = c
    c, d = up(c), down(d)
    a, b = add(second, ((0, 0), (1, 1)), (a, b), after=(after,))
    after = a
    a, b = up(a), down(b)
    c, d = add(near, ((0, 1), (1, 0)), (c, d), after=(after,))
    after = c
    c, d = up(c), down(d)
    a, b = add(near, ((0, 0), (1, 1)), (a, b), after=(after,))
    after = a
    a, b = up(a), down(b)
    row_old = hold(row_old, after)
    upper, lower = add(near, ((2, 0), (2, 1)), (d, c), after=(row_old,))
    grad = jnp.concatenate([upper + a, lower + b], axis=0)

    grad = lax.optimization_barrier(grad)
    row_own = jnp.concatenate([jnp.sum(grad * grad + 1e-30, axis=1), row_old[0]])
    row_other = lax.ppermute(row_own, "dp", SWAP)
    grad_other, row_other = lax.optimization_barrier((grad, row_other))
    grad_other = lax.ppermute(grad_other, "dp", SWAP)
    row_total = sum_four(jnp.concatenate([row_own[:ROWS], row_other[:ROWS]]), 2, (0, 1, 0))
    row_new = 0.8 * jnp.concatenate([row_own[ROWS:], row_other[ROWS:]]) + 0.2 * row_total / FF
    packed = []
    for weight in (None, 1.0 / row_new):
        sums = 0.0
        for g, rows in ((grad, slice(0, ROWS)), (grad_other, slice(ROWS, 2 * ROWS))):
            term = g * g + 1e-30 if weight is None else g * g * weight[rows, None]
            sums = sums + jnp.sum(term, axis=0)
        packed.append(sums)
    packed = jnp.concatenate([*packed, row_new])

    packed = sum_four(packed, 0, (0, 0, 1), (6, 7, 1))
    packed = packed + exchange(packed, (2, 0, 0), (0, 0, 1))
    packed = sum_four(packed, 1, (0, 0, 1))
    col_new = 0.8 * col_old + 0.2 * packed[:COLS] / D
    total = jnp.sum((packed[COLS:2 * COLS] / col_new).reshape(20, 128), axis=0)
    total = sum_four(total, 2, (0, 1, 0))
    core_one = jnp.bitwise_and(lax.axis_index("dp"), 1) == 1

    packed = jnp.concatenate([col_new, packed[2 * COLS:], total, row_new])
    other = lax.ppermute(packed, "dp", SWAP)
    row_new = jnp.where(core_one, packed[-2 * ROWS:-ROWS], other[-ROWS:])
    packed = jnp.where(core_one, packed, other)
    col_new, row_sum, total = packed[:COLS], packed[COLS:COLS + 128], packed[COLS + 128:COLS + 256]
    scaled = grad * lax.rsqrt(row_new[:, None] * col_new[None, :])
    update, update_rms = final(scaled, row_sum.reshape(1, 128), total.reshape(1, 128))
    return (update[None], row_new[None], col_new, update_rms.reshape(()))


def solution(mesh):
    return jax.shard_map(
        on_device,
        mesh=mesh,
        in_specs=(P("dp", None, "row", "col"), P("dp", "row"), P("col")),
        out_specs=(P("dp", "row", "col"), P("dp", "row"), P("col"), P()),
        check_vma=False,
    )
```

```python
import functools

import jax
import jax.numpy as jnp
from jax import lax
from jax.experimental import pallas as pl
from jax.experimental.pallas import tpu as pltpu
from jax.sharding import PartitionSpec as P

D = 4096
FF = 10240
HALF = 32
ROWS = 64
COLS = 2560

SWAP = [(i, i ^ 1) for i in range(16)]
UP = [(2 * z + c, 2 * ((z + 1 - 2 * c) % 8) + c) for z in range(8) for c in range(2)]
DOWN = [(j, i) for i, j in UP]

VMEM = pl.BlockSpec(memory_space=pltpu.VMEM)
HBM = pl.BlockSpec(memory_space=pltpu.HBM)
ANY = pl.BlockSpec(memory_space=pl.ANY)
PARAMS = pltpu.CompilerParams(vmem_limit_bytes=8 * 1024 * 1024)


def told(micros):
    return pl.CostEstimate(flops=int(micros * 1.15e9), bytes_accessed=0, transcendentals=0)


def fetch_kernel(ks, split, n_in, parts, *refs):
    own, *sent = refs[n_in:-3]
    buf, own_sems, sems = refs[-3:]
    height = ROWS // split
    me = lax.axis_index("dp")
    core = jnp.bitwise_and(me, 1)
    z = lax.shift_right_logical(me, 1) + 8
    own_copies, copies = [], []
    for i, k in enumerate(ks):
        step = k * (1 - 2 * core)
        here = 2 * jnp.bitwise_and(z + step, 7) + core
        there = 2 * jnp.bitwise_and(z - step, 7) + 1 - core
        copies.append(pltpu.make_async_copy(parts.at[there], buf.at[i], sems.at[i]))
        own_copies.append(pltpu.make_async_copy(parts.at[here], own.at[i], own_sems.at[i]))
    for copy in copies + own_copies:
        copy.start()
    for i, copy in enumerate(copies):
        copy.wait()
        for j in range(split):
            sent[j][i] = buf[i, j * height:(j + 1) * height].astype(jnp.float32)
    for copy in own_copies:
        copy.wait()


def fetch(ks, parts, *after, split=1, micros=0):
    n = len(ks)
    own, *sent = pl.pallas_call(
        functools.partial(fetch_kernel, ks, split, len(after)),
        out_shape=[jax.ShapeDtypeStruct((n, ROWS, COLS), jnp.bfloat16)]
        + [jax.ShapeDtypeStruct((n, ROWS // split, COLS), jnp.float32)] * split,
        in_specs=[HBM] + [ANY] * len(after),
        out_specs=[VMEM] * (1 + split),
        scratch_shapes=[
            pltpu.VMEM((n, ROWS, COLS), jnp.bfloat16),
            pltpu.SemaphoreType.DMA((n,)),
            pltpu.SemaphoreType.DMA((n,)),
        ],
        compiler_params=PARAMS,
        cost_estimate=told(micros),
    )(parts, *after)
    return own, *(lax.ppermute(x, "dp", SWAP) for x in sent)


def add_kernel(terms, n_in, own, sib, *refs):
    outs = refs[n_in:]
    for i, (block, half, has_state) in enumerate(terms):
        rows = slice(half * HALF, (half + 1) * HALF)
        other = sib[block, rows] if sib.shape[1] == ROWS else sib[block]
        total = own[block, rows].astype(jnp.float32) + other
        if has_state:
            total = total + refs[i][...]
        outs[i][...] = total


def add(blocks, terms, states=(), after=(), micros=12):
    return pl.pallas_call(
        functools.partial(add_kernel, [(*t, bool(states)) for t in terms], len(states) + len(after)),
        out_shape=[jax.ShapeDtypeStruct((HALF, COLS), jnp.float32)] * len(terms),
        in_specs=[VMEM] * (2 + len(states)) + [ANY] * len(after),
        out_specs=[VMEM] * len(terms),
        compiler_params=PARAMS,
        cost_estimate=told(micros),
    )(*blocks, *states, *after)


def hold_kernel(x, _, out):
    out[...] = x[...]


def hold(x, after):
    return pl.pallas_call(
        hold_kernel,
        out_shape=jax.ShapeDtypeStruct(x.shape, x.dtype),
        in_specs=[VMEM, ANY],
        out_specs=VMEM,
        compiler_params=PARAMS,
        cost_estimate=told(0),
    )(x, after)


def final_kernel(scaled, row_sum, total, out, rms, buf, sems):
    row_mean = jnp.sum(row_sum[...], keepdims=True) / D
    update_rms = jnp.sqrt(row_mean * jnp.sum(total[...], keepdims=True) / (D * FF))
    rms[...] = update_rms
    factor = jnp.sqrt(row_mean) / jnp.maximum(1.0, update_rms)
    copies = []
    for i in range(4):
        rows = pl.ds(16 * i, 16)
        buf[rows] = scaled[rows] * factor
        copies.append(pltpu.make_async_copy(buf.at[rows], out.at[rows], sems.at[i]))
        copies[i].start()
    for copy in copies:
        copy.wait()


def final(scaled, row_sum, total):
    return pl.pallas_call(
        final_kernel,
        out_shape=[
            jax.ShapeDtypeStruct((ROWS, COLS), jnp.float32),
            jax.ShapeDtypeStruct((1, 1), jnp.float32),
        ],
        in_specs=[VMEM, VMEM, VMEM],
        out_specs=[HBM, VMEM],
        scratch_shapes=[pltpu.VMEM((ROWS, COLS), jnp.float32), pltpu.SemaphoreType.DMA((4,))],
        compiler_params=PARAMS,
        cost_estimate=told(1),
    )(scaled, row_sum, total)


def places():
    return [(z, c, y, x) for z in range(8) for c in range(2) for y in range(4) for x in range(4)]


def number(z, c, y, x):
    return ((2 * z + c) * 4 + y) * 4 + x


def exchange(v, mask, idle=None):
    pairs = []
    for z, c, y, x in places():
        dz, dy, dx = mask if c == 1 or idle is None else idle
        pairs.append((number(z, c, y, x), number(z ^ dz, c, y ^ dy, x ^ dx)))
    return lax.ppermute(v, ("dp", "row", "col"), pairs)


def sum_four(v, axis, idle=None, masks=(1, 3, 2)):
    unit = [0, 0, 0]
    got = []
    for mask in masks:
        unit[axis] = mask
        got.append(exchange(v, tuple(unit), idle))
    return (got[0] + got[1]) + (got[2] + v)


def on_device(grad_parts, row_old, col_old):
    parts = pltpu.with_memory_space_constraint(grad_parts[0], pltpu.HBM)
    core_one = jnp.bitwise_and(lax.axis_index("dp"), 1) == 1

    def up(x):
        return lax.ppermute(x, "dp", UP)

    def down(x):
        return lax.ppermute(x, "dp", DOWN)

    far, far_up, far_down = fetch((4,), parts, split=2)
    third = fetch((3, -3), parts, far, micros=12)
    (a,) = add((far, far_up), ((0, 0),), after=(third[0],))
    after = a
    a = up(a)
    (b,) = add((far, far_down), ((0, 1),), after=(after,))
    after = b
    b = down(b)
    (c,) = add(third, ((0, 1),), after=(after,))
    (d,) = add(third, ((1, 0),), after=(c,))
    after = d
    second = fetch((2, -2), parts, after)
    near = fetch((1, -1, 0), parts, second[0])
    after = near[0]
    c, d = up(c), down(d)
    steps = [
        (third, (0, 0), (1, 1)),
        (second, (0, 1), (1, 0)),
        (second, (0, 0), (1, 1)),
        (near, (0, 1), (1, 0)),
        (near, (0, 0), (1, 1)),
    ]
    for blocks, first, last in steps:
        (x,) = add(blocks, (first,), (a,), after=(after,))
        (y,) = add(blocks, (last,), (b,), after=(x,))
        after = y
        a, b, c, d = c, d, up(x), down(y)
    a, b, c, d = c, d, a, b
    row_old = hold(row_old, after)
    upper, lower = add(near, ((2, 0), (2, 1)), (d, c), after=(row_old,))
    grad = jnp.concatenate([upper + a, lower + b], axis=0)

    grad = lax.optimization_barrier(grad)
    row_own = jnp.concatenate([jnp.sum(grad * grad + 1e-30, axis=1), row_old[0]])
    row_other = lax.ppermute(row_own, "dp", SWAP)
    grad_other, row_other = lax.optimization_barrier((grad, row_other))
    grad_other = lax.ppermute(grad_other, "dp", SWAP)
    row_total = sum_four(jnp.concatenate([row_own[:ROWS], row_other[:ROWS]]), 2, (0, 1, 0))
    row_new = 0.8 * jnp.concatenate([row_own[ROWS:], row_other[ROWS:]]) + 0.2 * row_total / FF
    packed = []
    for weight in (None, 1.0 / row_new):
        sums = 0.0
        for g, rows in ((grad, slice(0, ROWS)), (grad_other, slice(ROWS, 2 * ROWS))):
            term = g * g + 1e-30 if weight is None else g * g * weight[rows, None]
            sums = sums + jnp.sum(term, axis=0)
        packed.append(sums)
    packed = jnp.concatenate([*packed, row_new])

    packed = sum_four(packed, 0, (0, 0, 1), (1, 7, 6))
    packed = packed + exchange(packed, (2, 0, 0), (0, 0, 1))
    packed = sum_four(packed, 1, (0, 0, 1))
    col_new = 0.8 * col_old + 0.2 * packed[:COLS] / D
    total = jnp.sum((packed[COLS:2 * COLS] / col_new).reshape(20, 128), axis=0)
    total = sum_four(total, 2, (0, 1, 0))
    core_one = jnp.bitwise_and(lax.axis_index("dp"), 1) == 1

    packed = jnp.concatenate([col_new, packed[2 * COLS:], total, row_new])
    other = lax.ppermute(packed, "dp", SWAP)
    row_new = jnp.where(core_one, packed[-2 * ROWS:-ROWS], other[-ROWS:])
    packed = jnp.where(core_one, packed, other)
    col_new, row_sum, total = packed[:COLS], packed[COLS:COLS + 128], packed[COLS + 128:COLS + 256]
    scaled = grad * lax.rsqrt(row_new[:, None] * col_new[None, :])
    update, update_rms = final(scaled, row_sum.reshape(1, 128), total.reshape(1, 128))
    return (update[None], row_new[None], col_new, update_rms.reshape(()))


def solution(mesh):
    return jax.shard_map(
        on_device,
        mesh=mesh,
        in_specs=(P("dp", None, "row", "col"), P("dp", "row"), P("col")),
        out_specs=(P("dp", "row", "col"), P("dp", "row"), P("col"), P()),
        check_vma=False,
    )
```

```python
import functools

import jax
import jax.numpy as jnp
from jax import lax
from jax.experimental import pallas as pl
from jax.experimental.pallas import tpu as pltpu
from jax.sharding import PartitionSpec as P

D = 4096
FF = 10240
HALF = 32
ROWS = 64
COLS = 2560

SWAP = [(i, i ^ 1) for i in range(16)]
UP = [(2 * z + c, 2 * ((z + 1 - 2 * c) % 8) + c) for z in range(8) for c in range(2)]
DOWN = [(j, i) for i, j in UP]

VMEM = pl.BlockSpec(memory_space=pltpu.VMEM)
HBM = pl.BlockSpec(memory_space=pltpu.HBM)
ANY = pl.BlockSpec(memory_space=pl.ANY)
PARAMS = pltpu.CompilerParams(vmem_limit_bytes=8 * 1024 * 1024)


def told(micros):
    return pl.CostEstimate(flops=int(micros * 1.15e9), bytes_accessed=0, transcendentals=0)


def fetch_kernel(ks, split, n_in, parts, *refs):
    own, *sent = refs[n_in:-3]
    buf, own_sems, sems = refs[-3:]
    height = ROWS // split
    me = lax.axis_index("dp")
    core = jnp.bitwise_and(me, 1)
    z = lax.shift_right_logical(me, 1) + 8
    own_copies, copies = [], []
    for i, k in enumerate(ks):
        step = k * (1 - 2 * core)
        here = 2 * jnp.bitwise_and(z + step, 7) + core
        there = 2 * jnp.bitwise_and(z - step, 7) + 1 - core
        copies.append(pltpu.make_async_copy(parts.at[there], buf.at[i], sems.at[i]))
        own_copies.append(pltpu.make_async_copy(parts.at[here], own.at[i], own_sems.at[i]))
    for copy in copies + own_copies:
        copy.start()
    for i, copy in enumerate(copies):
        copy.wait()
        for j in range(split):
            sent[j][i] = buf[i, j * height:(j + 1) * height].astype(jnp.float32)
    for copy in own_copies:
        copy.wait()


def fetch(ks, parts, *after, split=1, micros=0):
    n = len(ks)
    own, *sent = pl.pallas_call(
        functools.partial(fetch_kernel, ks, split, len(after)),
        out_shape=[jax.ShapeDtypeStruct((n, ROWS, COLS), jnp.bfloat16)]
        + [jax.ShapeDtypeStruct((n, ROWS // split, COLS), jnp.float32)] * split,
        in_specs=[HBM] + [ANY] * len(after),
        out_specs=[VMEM] * (1 + split),
        scratch_shapes=[
            pltpu.VMEM((n, ROWS, COLS), jnp.bfloat16),
            pltpu.SemaphoreType.DMA((n,)),
            pltpu.SemaphoreType.DMA((n,)),
        ],
        compiler_params=PARAMS,
        cost_estimate=told(micros),
    )(parts, *after)
    return own, *(lax.ppermute(x, "dp", SWAP) for x in sent)


def add_kernel(terms, n_in, own, sib, *refs):
    outs = refs[n_in:]
    for i, (block, half, has_state) in enumerate(terms):
        rows = slice(half * HALF, (half + 1) * HALF)
        other = sib[block, rows] if sib.shape[1] == ROWS else sib[block]
        total = own[block, rows].astype(jnp.float32) + other
        if has_state:
            total = total + refs[i][...]
        outs[i][...] = total


def add(blocks, terms, states=(), after=(), micros=12):
    return pl.pallas_call(
        functools.partial(add_kernel, [(*t, bool(states)) for t in terms], len(states) + len(after)),
        out_shape=[jax.ShapeDtypeStruct((HALF, COLS), jnp.float32)] * len(terms),
        in_specs=[VMEM] * (2 + len(states)) + [ANY] * len(after),
        out_specs=[VMEM] * len(terms),
        compiler_params=PARAMS,
        cost_estimate=told(micros),
    )(*blocks, *states, *after)


def hold_kernel(x, _, out):
    out[...] = x[...]


def hold(x, after):
    return pl.pallas_call(
        hold_kernel,
        out_shape=jax.ShapeDtypeStruct(x.shape, x.dtype),
        in_specs=[VMEM, ANY],
        out_specs=VMEM,
        compiler_params=PARAMS,
        cost_estimate=told(0),
    )(x, after)


def final_kernel(scaled, row_sum, total, out, rms, buf, sems):
    row_mean = jnp.sum(row_sum[...], keepdims=True) / D
    update_rms = jnp.sqrt(row_mean * jnp.sum(total[...], keepdims=True) / (D * FF))
    rms[...] = update_rms
    factor = jnp.sqrt(row_mean) / jnp.maximum(1.0, update_rms)
    copies = []
    for i in range(4):
        rows = pl.ds(16 * i, 16)
        buf[rows] = scaled[rows] * factor
        copies.append(pltpu.make_async_copy(buf.at[rows], out.at[rows], sems.at[i]))
        copies[i].start()
    for copy in copies:
        copy.wait()


def final(scaled, row_sum, total):
    return pl.pallas_call(
        final_kernel,
        out_shape=[
            jax.ShapeDtypeStruct((ROWS, COLS), jnp.float32),
            jax.ShapeDtypeStruct((1, 1), jnp.float32),
        ],
        in_specs=[VMEM, VMEM, VMEM],
        out_specs=[HBM, VMEM],
        scratch_shapes=[pltpu.VMEM((ROWS, COLS), jnp.float32), pltpu.SemaphoreType.DMA((4,))],
        compiler_params=PARAMS,
        cost_estimate=told(1),
    )(scaled, row_sum, total)


def places():
    return [(z, c, y, x) for z in range(8) for c in range(2) for y in range(4) for x in range(4)]


def number(z, c, y, x):
    return ((2 * z + c) * 4 + y) * 4 + x


def exchange(v, mask, idle=None):
    pairs = []
    for z, c, y, x in places():
        dz, dy, dx = mask if c == 1 or idle is None else idle
        pairs.append((number(z, c, y, x), number(z ^ dz, c, y ^ dy, x ^ dx)))
    return lax.ppermute(v, ("dp", "row", "col"), pairs)


def sum_four(v, axis, idle=None, masks=(1, 3, 2)):
    unit = [0, 0, 0]
    got = []
    for mask in masks:
        unit[axis] = mask
        got.append(exchange(v, tuple(unit), idle))
    return (got[0] + got[1]) + (got[2] + v)


def on_device(grad_parts, row_old, col_old):
    parts = pltpu.with_memory_space_constraint(grad_parts[0], pltpu.HBM)
    core_one = jnp.bitwise_and(lax.axis_index("dp"), 1) == 1

    def up(x):
        return lax.ppermute(x, "dp", UP)

    def down(x):
        return lax.ppermute(x, "dp", DOWN)

    far, far_up, far_down = fetch((4,), parts, split=2)
    third = fetch((3, -3), parts, far, micros=12)
    (a,) = add((far, far_up), ((0, 0),), after=(third[0],))
    after = a
    a = up(a)
    (b,) = add((far, far_down), ((0, 1),), after=(after,))
    after = b
    b = down(b)
    (c,) = add(third, ((0, 1),), after=(after,))
    (d,) = add(third, ((1, 0),), after=(c,))
    after = d
    second = fetch((2, -2), parts, after)
    near = fetch((1, -1, 0), parts, second[0])
    after = near[0]
    c, d = up(c), down(d)
    steps = [
        (third, (0, 0), (1, 1)),
        (second, (0, 1), (1, 0)),
        (second, (0, 0), (1, 1)),
        (near, (0, 1), (1, 0)),
        (near, (0, 0), (1, 1)),
    ]
    for blocks, first, last in steps:
        (x,) = add(blocks, (first,), (a,), after=(after,))
        (y,) = add(blocks, (last,), (b,), after=(x,))
        after = y
        a, b, c, d = c, d, up(x), down(y)
    a, b, c, d = c, d, a, b
    row_old = hold(row_old, after)
    upper, lower = add(near, ((2, 0), (2, 1)), (d, c), after=(row_old,))
    grad = jnp.concatenate([upper + a, lower + b], axis=0)

    grad = lax.optimization_barrier(grad)
    row_own = jnp.concatenate([jnp.sum(grad * grad + 1e-30, axis=1), row_old[0]])
    row_other = lax.ppermute(row_own, "dp", SWAP)
    grad_other, row_other = lax.optimization_barrier((grad, row_other))
    grad_other = lax.ppermute(grad_other, "dp", SWAP)
    row_total = sum_four(jnp.concatenate([row_own[:ROWS], row_other[:ROWS]]), 2, (0, 1, 0))
    row_new = 0.8 * jnp.concatenate([row_own[ROWS:], row_other[ROWS:]]) + 0.2 * row_total / FF
    packed = []
    for weight in (None, 1.0 / row_new):
        sums = 0.0
        for g, rows in ((grad, slice(0, ROWS)), (grad_other, slice(ROWS, 2 * ROWS))):
            term = g * g + 1e-30 if weight is None else g * g * weight[rows, None]
            sums = sums + jnp.sum(term, axis=0)
        packed.append(sums)
    packed = jnp.concatenate([*packed, row_new])

    packed = sum_four(packed, 0, (0, 0, 1))
    packed = packed + exchange(packed, (7, 0, 0), (0, 0, 1))
    packed = sum_four(packed, 1, (0, 0, 1))
    col_new = 0.8 * col_old + 0.2 * packed[:COLS] / D
    total = jnp.sum((packed[COLS:2 * COLS] / col_new).reshape(20, 128), axis=0)
    total = sum_four(total, 2, (0, 1, 0))
    core_one = jnp.bitwise_and(lax.axis_index("dp"), 1) == 1

    packed = jnp.concatenate([col_new, packed[2 * COLS:], total, row_new])
    other = lax.ppermute(packed, "dp", SWAP)
    row_new = jnp.where(core_one, packed[-2 * ROWS:-ROWS], other[-ROWS:])
    packed = jnp.where(core_one, packed, other)
    col_new, row_sum, total = packed[:COLS], packed[COLS:COLS + 128], packed[COLS + 128:COLS + 256]
    scaled = grad * lax.rsqrt(row_new[:, None] * col_new[None, :])
    update, update_rms = final(scaled, row_sum.reshape(1, 128), total.reshape(1, 128))
    return (update[None], row_new[None], col_new, update_rms.reshape(()))


def solution(mesh):
    return jax.shard_map(
        on_device,
        mesh=mesh,
        in_specs=(P("dp", None, "row", "col"), P("dp", "row"), P("col")),
        out_specs=(P("dp", "row", "col"), P("dp", "row"), P("col"), P()),
        check_vma=False,
    )
```

```python
import functools

import jax
import jax.numpy as jnp
from jax import lax
from jax.experimental import pallas as pl
from jax.experimental.pallas import tpu as pltpu
from jax.sharding import PartitionSpec as P

D = 4096
FF = 10240
HALF = 32
ROWS = 64
COLS = 2560

SWAP = [(i, i ^ 1) for i in range(16)]
UP = [(2 * z + c, 2 * ((z + 1 - 2 * c) % 8) + c) for z in range(8) for c in range(2)]
DOWN = [(j, i) for i, j in UP]

VMEM = pl.BlockSpec(memory_space=pltpu.VMEM)
HBM = pl.BlockSpec(memory_space=pltpu.HBM)
ANY = pl.BlockSpec(memory_space=pl.ANY)
PARAMS = pltpu.CompilerParams(vmem_limit_bytes=8 * 1024 * 1024)


def told(micros):
    return pl.CostEstimate(flops=int(micros * 1.15e9), bytes_accessed=0, transcendentals=0)


def fetch_kernel(ks, split, n_in, parts, *refs):
    own, *sent = refs[n_in:-3]
    buf, own_sems, sems = refs[-3:]
    height = ROWS // split
    me = lax.axis_index("dp")
    core = jnp.bitwise_and(me, 1)
    z = lax.shift_right_logical(me, 1) + 8
    own_copies, copies = [], []
    for i, k in enumerate(ks):
        step = k * (1 - 2 * core)
        here = 2 * jnp.bitwise_and(z + step, 7) + core
        there = 2 * jnp.bitwise_and(z - step, 7) + 1 - core
        copies.append(pltpu.make_async_copy(parts.at[there], buf.at[i], sems.at[i]))
        own_copies.append(pltpu.make_async_copy(parts.at[here], own.at[i], own_sems.at[i]))
    for copy in copies + own_copies:
        copy.start()
    for i, copy in enumerate(copies):
        copy.wait()
        for j in range(split):
            sent[j][i] = buf[i, j * height:(j + 1) * height].astype(jnp.float32)
    for copy in own_copies:
        copy.wait()


def fetch(ks, parts, *after, split=1, micros=0):
    n = len(ks)
    own, *sent = pl.pallas_call(
        functools.partial(fetch_kernel, ks, split, len(after)),
        out_shape=[jax.ShapeDtypeStruct((n, ROWS, COLS), jnp.bfloat16)]
        + [jax.ShapeDtypeStruct((n, ROWS // split, COLS), jnp.float32)] * split,
        in_specs=[HBM] + [ANY] * len(after),
        out_specs=[VMEM] * (1 + split),
        scratch_shapes=[
            pltpu.VMEM((n, ROWS, COLS), jnp.bfloat16),
            pltpu.SemaphoreType.DMA((n,)),
            pltpu.SemaphoreType.DMA((n,)),
        ],
        compiler_params=PARAMS,
        cost_estimate=told(micros),
    )(parts, *after)
    return own, *(lax.ppermute(x, "dp", SWAP) for x in sent)


def add_kernel(terms, n_in, own, sib, *refs):
    outs = refs[n_in:]
    for i, (block, half, has_state) in enumerate(terms):
        rows = slice(half * HALF, (half + 1) * HALF)
        other = sib[block, rows] if sib.shape[1] == ROWS else sib[block]
        total = own[block, rows].astype(jnp.float32) + other
        if has_state:
            total = total + refs[i][...]
        outs[i][...] = total


def add(blocks, terms, states=(), after=(), micros=12):
    return pl.pallas_call(
        functools.partial(add_kernel, [(*t, bool(states)) for t in terms], len(states) + len(after)),
        out_shape=[jax.ShapeDtypeStruct((HALF, COLS), jnp.float32)] * len(terms),
        in_specs=[VMEM] * (2 + len(states)) + [ANY] * len(after),
        out_specs=[VMEM] * len(terms),
        compiler_params=PARAMS,
        cost_estimate=told(micros),
    )(*blocks, *states, *after)


def hold_kernel(x, _, out):
    out[...] = x[...]


def hold(x, after):
    return pl.pallas_call(
        hold_kernel,
        out_shape=jax.ShapeDtypeStruct(x.shape, x.dtype),
        in_specs=[VMEM, ANY],
        out_specs=VMEM,
        compiler_params=PARAMS,
        cost_estimate=told(0),
    )(x, after)


def final_kernel(scaled, row_sum, total, out, rms, buf, sems):
    row_mean = jnp.sum(row_sum[...], keepdims=True) / D
    update_rms = jnp.sqrt(row_mean * jnp.sum(total[...], keepdims=True) / (D * FF))
    rms[...] = update_rms
    factor = jnp.sqrt(row_mean) / jnp.maximum(1.0, update_rms)
    copies = []
    for i in range(4):
        rows = pl.ds(16 * i, 16)
        buf[rows] = scaled[rows] * factor
        copies.append(pltpu.make_async_copy(buf.at[rows], out.at[rows], sems.at[i]))
        copies[i].start()
    for copy in copies:
        copy.wait()


def final(scaled, row_sum, total):
    return pl.pallas_call(
        final_kernel,
        out_shape=[
            jax.ShapeDtypeStruct((ROWS, COLS), jnp.float32),
            jax.ShapeDtypeStruct((1, 1), jnp.float32),
        ],
        in_specs=[VMEM, VMEM, VMEM],
        out_specs=[HBM, VMEM],
        scratch_shapes=[pltpu.VMEM((ROWS, COLS), jnp.float32), pltpu.SemaphoreType.DMA((4,))],
        compiler_params=PARAMS,
        cost_estimate=told(1),
    )(scaled, row_sum, total)


def places():
    return [(z, c, y, x) for z in range(8) for c in range(2) for y in range(4) for x in range(4)]


def number(z, c, y, x):
    return ((2 * z + c) * 4 + y) * 4 + x


def exchange(v, mask, idle=None):
    pairs = []
    for z, c, y, x in places():
        dz, dy, dx = mask if c == 1 or idle is None else idle
        pairs.append((number(z, c, y, x), number(z ^ dz, c, y ^ dy, x ^ dx)))
    return lax.ppermute(v, ("dp", "row", "col"), pairs)


def sum_four(v, axis, idle=None, masks=(1, 3, 2)):
    unit = [0, 0, 0]
    got = []
    for mask in masks:
        unit[axis] = mask
        got.append(exchange(v, tuple(unit), idle))
    return (got[0] + got[1]) + (got[2] + v)


def on_device(grad_parts, row_old, col_old):
    parts = pltpu.with_memory_space_constraint(grad_parts[0], pltpu.HBM)
    core_one = jnp.bitwise_and(lax.axis_index("dp"), 1) == 1

    def up(x):
        return lax.ppermute(x, "dp", UP)

    def down(x):
        return lax.ppermute(x, "dp", DOWN)

    far, far_up, far_down = fetch((4,), parts, split=2)
    third = fetch((3, -3), parts, far, micros=12)
    (a,) = add((far, far_up), ((0, 0),), after=(third[0],))
    after = a
    a = up(a)
    (b,) = add((far, far_down), ((0, 1),), after=(after,))
    after = b
    b = down(b)
    (c,) = add(third, ((0, 1),), after=(after,))
    (d,) = add(third, ((1, 0),), after=(c,))
    after = d
    second = fetch((2, -2), parts, after)
    near = fetch((1, -1, 0), parts, second[0])
    after = near[0]
    c, d = up(c), down(d)
    steps = [
        (third, (0, 0), (1, 1)),
        (second, (0, 1), (1, 0)),
        (second, (0, 0), (1, 1)),
        (near, (0, 1), (1, 0)),
        (near, (0, 0), (1, 1)),
    ]
    for blocks, first, last in steps:
        (x,) = add(blocks, (first,), (a,), after=(after,))
        (y,) = add(blocks, (last,), (b,), after=(x,))
        after = y
        a, b, c, d = c, d, up(x), down(y)
    a, b, c, d = c, d, a, b
    row_old = hold(row_old, after)
    upper, lower = add(near, ((2, 0), (2, 1)), (d, c), after=(row_old,))
    grad = jnp.concatenate([upper + a, lower + b], axis=0)

    grad = lax.optimization_barrier(grad)
    row_own = jnp.concatenate([jnp.sum(grad * grad + 1e-30, axis=1), row_old[0]])
    row_other = lax.ppermute(row_own, "dp", SWAP)
    grad_other, row_other = lax.optimization_barrier((grad, row_other))
    grad_other = lax.ppermute(grad_other, "dp", SWAP)
    row_total = sum_four(jnp.concatenate([row_own[:ROWS], row_other[:ROWS]]), 2, (0, 1, 0))
    row_new = 0.8 * jnp.concatenate([row_own[ROWS:], row_other[ROWS:]]) + 0.2 * row_total / FF
    packed = []
    for weight in (None, 1.0 / row_new):
        sums = 0.0
        for g, rows in ((grad, slice(0, ROWS)), (grad_other, slice(ROWS, 2 * ROWS))):
            term = g * g + 1e-30 if weight is None else g * g * weight[rows, None]
            sums = sums + jnp.sum(term, axis=0)
        packed.append(sums)
    packed = jnp.concatenate([*packed, row_new])

    packed = packed + exchange(packed, (7, 0, 0), (0, 0, 1))
    packed = sum_four(packed, 0, (0, 0, 1))
    packed = sum_four(packed, 1, (0, 0, 1))
    col_new = 0.8 * col_old + 0.2 * packed[:COLS] / D
    total = jnp.sum((packed[COLS:2 * COLS] / col_new).reshape(20, 128), axis=0)
    total = sum_four(total, 2, (0, 1, 0))
    core_one = jnp.bitwise_and(lax.axis_index("dp"), 1) == 1

    packed = jnp.concatenate([col_new, packed[2 * COLS:], total, row_new])
    other = lax.ppermute(packed, "dp", SWAP)
    row_new = jnp.where(core_one, packed[-2 * ROWS:-ROWS], other[-ROWS:])
    packed = jnp.where(core_one, packed, other)
    col_new, row_sum, total = packed[:COLS], packed[COLS:COLS + 128], packed[COLS + 128:COLS + 256]
    scaled = grad * lax.rsqrt(row_new[:, None] * col_new[None, :])
    update, update_rms = final(scaled, row_sum.reshape(1, 128), total.reshape(1, 128))
    return (update[None], row_new[None], col_new, update_rms.reshape(()))


def solution(mesh):
    return jax.shard_map(
        on_device,
        mesh=mesh,
        in_specs=(P("dp", None, "row", "col"), P("dp", "row"), P("col")),
        out_specs=(P("dp", "row", "col"), P("dp", "row"), P("col"), P()),
        check_vma=False,
    )
```

```python
import functools

import jax
import jax.numpy as jnp
from jax import lax
from jax.experimental import pallas as pl
from jax.experimental.pallas import tpu as pltpu
from jax.sharding import PartitionSpec as P

D = 4096
FF = 10240
HALF = 32
ROWS = 64
COLS = 2560

SWAP = [(i, i ^ 1) for i in range(16)]
UP = [(2 * z + c, 2 * ((z + 1 - 2 * c) % 8) + c) for z in range(8) for c in range(2)]
DOWN = [(j, i) for i, j in UP]

VMEM = pl.BlockSpec(memory_space=pltpu.VMEM)
HBM = pl.BlockSpec(memory_space=pltpu.HBM)
ANY = pl.BlockSpec(memory_space=pl.ANY)
PARAMS = pltpu.CompilerParams(vmem_limit_bytes=8 * 1024 * 1024)


def told(micros):
    return pl.CostEstimate(flops=int(micros * 1.15e9), bytes_accessed=0, transcendentals=0)


def swap(x):
    return lax.ppermute(x, "dp", SWAP)


def fetch_kernel(ks, split, n_in, parts, *refs):
    own, *sent = refs[n_in:-3]
    buf, own_sems, sems = refs[-3:]
    height = ROWS // split
    me = lax.axis_index("dp")
    core = jnp.bitwise_and(me, 1)
    z = lax.shift_right_logical(me, 1) + 8
    own_copies, copies = [], []
    for i, k in enumerate(ks):
        step = k * (1 - 2 * core)
        here = 2 * jnp.bitwise_and(z + step, 7) + core
        there = 2 * jnp.bitwise_and(z - step, 7) + 1 - core
        copies.append(pltpu.make_async_copy(parts.at[there], buf.at[i], sems.at[i]))
        own_copies.append(pltpu.make_async_copy(parts.at[here], own.at[i], own_sems.at[i]))
    for copy in copies + own_copies:
        copy.start()
    for i, copy in enumerate(copies):
        copy.wait()
        for j in range(split):
            sent[j][i] = buf[i, j * height:(j + 1) * height].astype(jnp.float32)
    for copy in own_copies:
        copy.wait()


def fetch(ks, parts, *after, split=1, micros=0):
    n = len(ks)
    own, *sent = pl.pallas_call(
        functools.partial(fetch_kernel, ks, split, len(after)),
        out_shape=[jax.ShapeDtypeStruct((n, ROWS, COLS), jnp.bfloat16)]
        + [jax.ShapeDtypeStruct((n, ROWS // split, COLS), jnp.float32)] * split,
        in_specs=[HBM] + [ANY] * len(after),
        out_specs=[VMEM] * (1 + split),
        scratch_shapes=[
            pltpu.VMEM((n, ROWS, COLS), jnp.bfloat16),
            pltpu.SemaphoreType.DMA((n,)),
            pltpu.SemaphoreType.DMA((n,)),
        ],
        compiler_params=PARAMS,
        cost_estimate=told(micros),
    )(parts, *after)
    return own, *sent


def add_kernel(terms, n_in, own, sib, *refs):
    outs = refs[n_in:]
    for i, (block, half, has_state) in enumerate(terms):
        rows = slice(half * HALF, (half + 1) * HALF)
        other = sib[block, rows] if sib.shape[1] == ROWS else sib[block]
        total = own[block, rows].astype(jnp.float32) + other
        if has_state:
            total = total + refs[i][...]
        outs[i][...] = total


def add(blocks, terms, states=(), after=(), micros=12):
    return pl.pallas_call(
        functools.partial(add_kernel, [(*t, bool(states)) for t in terms], len(states) + len(after)),
        out_shape=[jax.ShapeDtypeStruct((HALF, COLS), jnp.float32)] * len(terms),
        in_specs=[VMEM] * (2 + len(states)) + [ANY] * len(after),
        out_specs=[VMEM] * len(terms),
        compiler_params=PARAMS,
        cost_estimate=told(micros),
    )(*blocks, *states, *after)


def hold_kernel(x, _, out):
    out[...] = x[...]


def hold(x, after):
    return pl.pallas_call(
        hold_kernel,
        out_shape=jax.ShapeDtypeStruct(x.shape, x.dtype),
        in_specs=[VMEM, ANY],
        out_specs=VMEM,
        compiler_params=PARAMS,
        cost_estimate=told(0),
    )(x, after)


def final_kernel(scaled, row_sum, total, out, rms, buf, sems):
    row_mean = jnp.sum(row_sum[...], keepdims=True) / D
    update_rms = jnp.sqrt(row_mean * jnp.sum(total[...], keepdims=True) / (D * FF))
    rms[...] = update_rms
    factor = jnp.sqrt(row_mean) / jnp.maximum(1.0, update_rms)
    copies = []
    for i in range(8):
        rows = pl.ds(8 * i, 8)
        buf[rows] = scaled[rows] * factor
        copies.append(pltpu.make_async_copy(buf.at[rows], out.at[rows], sems.at[i]))
        copies[i].start()
    for copy in copies:
        copy.wait()


def final(scaled, row_sum, total):
    return pl.pallas_call(
        final_kernel,
        out_shape=[
            jax.ShapeDtypeStruct((ROWS, COLS), jnp.float32),
            jax.ShapeDtypeStruct((1, 1), jnp.float32),
        ],
        in_specs=[VMEM, VMEM, VMEM],
        out_specs=[HBM, VMEM],
        scratch_shapes=[pltpu.VMEM((ROWS, COLS), jnp.float32), pltpu.SemaphoreType.DMA((8,))],
        compiler_params=PARAMS,
        cost_estimate=told(1),
    )(scaled, row_sum, total)


def places():
    return [(z, c, y, x) for z in range(8) for c in range(2) for y in range(4) for x in range(4)]


def number(z, c, y, x):
    return ((2 * z + c) * 4 + y) * 4 + x


def exchange(v, mask, idle=None):
    pairs = []
    for z, c, y, x in places():
        dz, dy, dx = mask if c == 1 or idle is None else idle
        pairs.append((number(z, c, y, x), number(z ^ dz, c, y ^ dy, x ^ dx)))
    return lax.ppermute(v, ("dp", "row", "col"), pairs)


def sum_four(v, axis, idle=None, masks=(1, 3, 2)):
    unit = [0, 0, 0]
    got = []
    for mask in masks:
        unit[axis] = mask
        got.append(exchange(v, tuple(unit), idle))
    return (got[0] + got[1]) + (got[2] + v)


def on_device(grad_parts, row_old, col_old):
    parts = pltpu.with_memory_space_constraint(grad_parts[0], pltpu.HBM)
    core_one = jnp.bitwise_and(lax.axis_index("dp"), 1) == 1

    def up(x):
        return lax.ppermute(x, "dp", UP)

    def down(x):
        return lax.ppermute(x, "dp", DOWN)

    far, *sent = fetch((4,), parts, split=2)
    far_up, far_down = (swap(x) for x in sent)
    third = fetch((3, -3), parts, far, micros=12)
    (a,) = add((far, far_up), ((0, 0),), after=(third[0],))
    sent, a = lax.optimization_barrier((third[1], a))
    third = third[0], swap(sent)
    after = a
    a = up(a)
    (b,) = add((far, far_down), ((0, 1),), after=(after,))
    after = b
    b = down(b)
    (c,) = add(third, ((0, 1),), after=(after,))
    (d,) = add(third, ((1, 0),), after=(c,))
    after = d
    own, sent = fetch((2, -2), parts, after)
    second = own, swap(sent)
    own, sent = fetch((1, -1, 0), parts, second[0])
    near = own, swap(sent)
    after = near[0]
    c, d = up(c), down(d)
    steps = [
        (third, (0, 0), (1, 1)),
        (second, (0, 1), (1, 0)),
        (second, (0, 0), (1, 1)),
        (near, (0, 1), (1, 0)),
        (near, (0, 0), (1, 1)),
    ]
    for blocks, first, last in steps:
        (x,) = add(blocks, (first,), (a,), after=(after,))
        (y,) = add(blocks, (last,), (b,), after=(x,))
        after = y
        a, b, c, d = c, d, up(x), down(y)
    a, b, c, d = c, d, a, b
    row_old = hold(row_old, after)
    upper, lower = add(near, ((2, 0), (2, 1)), (d, c), after=(row_old,))
    grad = jnp.concatenate([upper + a, lower + b], axis=0)

    grad = lax.optimization_barrier(grad)
    row_own = jnp.concatenate([jnp.sum(grad * grad + 1e-30, axis=1), row_old[0]])
    row_other = lax.ppermute(row_own, "dp", SWAP)
    grad_other, row_other = lax.optimization_barrier((grad, row_other))
    grad_other = lax.ppermute(grad_other, "dp", SWAP)
    row_total = sum_four(jnp.concatenate([row_own[:ROWS], row_other[:ROWS]]), 2, (0, 1, 0))
    row_new = 0.8 * jnp.concatenate([row_own[ROWS:], row_other[ROWS:]]) + 0.2 * row_total / FF
    packed = []
    for weight in (None, 1.0 / row_new):
        sums = 0.0
        for g, rows in ((grad, slice(0, ROWS)), (grad_other, slice(ROWS, 2 * ROWS))):
            term = g * g + 1e-30 if weight is None else g * g * weight[rows, None]
            sums = sums + jnp.sum(term, axis=0)
        packed.append(sums)
    packed = jnp.concatenate([*packed, row_new])

    packed = sum_four(packed, 0, (0, 0, 1))
    packed = packed + exchange(packed, (7, 0, 0), (0, 0, 1))
    packed = sum_four(packed, 1, (0, 0, 1))
    col_new = 0.8 * col_old + 0.2 * packed[:COLS] / D
    total = jnp.sum((packed[COLS:2 * COLS] / col_new).reshape(20, 128), axis=0)
    total = sum_four(total, 2, (0, 1, 0))
    core_one = jnp.bitwise_and(lax.axis_index("dp"), 1) == 1

    packed = jnp.concatenate([col_new, packed[2 * COLS:], total, row_new])
    other = lax.ppermute(packed, "dp", SWAP)
    row_new = jnp.where(core_one, packed[-2 * ROWS:-ROWS], other[-ROWS:])
    packed = jnp.where(core_one, packed, other)
    col_new, row_sum, total = packed[:COLS], packed[COLS:COLS + 128], packed[COLS + 128:COLS + 256]
    scaled = grad * lax.rsqrt(row_new[:, None] * col_new[None, :])
    update, update_rms = final(scaled, row_sum.reshape(1, 128), total.reshape(1, 128))
    return (update[None], row_new[None], col_new, update_rms.reshape(()))


def solution(mesh):
    return jax.shard_map(
        on_device,
        mesh=mesh,
        in_specs=(P("dp", None, "row", "col"), P("dp", "row"), P("col")),
        out_specs=(P("dp", "row", "col"), P("dp", "row"), P("col"), P()),
        check_vma=False,
    )
```
